32 devices in a mesh: dp: 4 (over y, x), expert: 8 (over z, core).
Axes of the slice: x: 2, y: 2, z: 4, core: 2. Of those that a mesh axis runs over, the one named last changes fastest.
Arguments:
- grad_out: bfloat16 [4096, 5120], P(('dp', 'expert')), may hold values from -6 to 6
- expert_ids: int32 [4096, 1], P(('dp', 'expert')), may hold values from 0 to 7; in each aligned block of 128 rows (0 to 127, 128 to 255, ...) at most 20 rows name the same one
- gate_weights: bfloat16 [4096], P(('dp', 'expert')), may hold values from 0.099609375 to 1
- saved_hidden: bfloat16 [8, 640, 8192], P('expert', None, 'dp'), may hold values from -0.06591797 to 0.06591797
- down_weight: bfloat16 [8, 8192, 5120], P('expert', 'dp'), may hold values from -0.0625 to 0.0625
Outputs:
- grad_hidden: bfloat16 [8, 640, 8192], P('expert', None, 'dp')
- grad_gate: float32 [4096], P(('dp', 'expert'))
The draws below stay inside these ranges and needn't reach their ends.
Inputs may be any that keep to these rules, and one draw needn't show every extreme that they name: `expert_ids`: within the 128 tokens of one device no expert is named more than 20 times, and in every draw some expert is named exactly 20 times by some device's tokens.
All inputs are finite; a program needn't handle non-finite values.
Results may differ from the reference program's by a relative error of at most 0.001.
Values may be sent and summed in bfloat16 or wider, within the bound.
A program may use at most 192 MiB of HBM per device.

```python
import math
import jax
import jax.numpy as jnp
import numpy as np
from jax import lax

D = 5120
FF = 8192
TOK_DEV = 128
EXPERTS = 8
MOST = 20
TOKENS = 4096
SLOTS = 640


def steps_of(rng, dims, cuts, least, largest):
    loudness = 1.0
    for axis_at, blocks in cuts:
        draws = jax.random.uniform(jax.random.fold_in(jax.random.fold_in(rng, 6), axis_at), (blocks,), jnp.float32, least / len(cuts), largest / len(cuts))
        loudness = loudness * jnp.repeat(jnp.exp(draws), dims[axis_at] // blocks).reshape((-1,) + (1,) * (len(dims) - 1 - axis_at))
    return loudness


def shared_out(key, own, number, rows, number_of, top, bound, slope):
    sequence = jax.random.permutation(key, number_of)
    crowded, common = shares(number_of, rows * top, bound, slope, True), shares(number_of, rows * top, bound, slope, False)
    places = jnp.arange(number_of)

    def named(lengths, rotation):
        used = int((lengths > 0).sum())
        fixed = max(1, used // 4)
        passed = fixed + (places - fixed + rotation * (used - fixed)) % max(1, number_of - fixed)
        return jnp.zeros((number_of,), jnp.int32).at[sequence[jnp.where(places < fixed, places, passed)]].set(jnp.asarray(lengths, jnp.int32))

    lengths = jnp.where(number % 4 == 0, named(crowded, number // 4), named(common, number - number // 4 - 1))
    mixed = jax.random.permutation(jax.random.fold_in(own, 3), number_of)
    donor, receiver = mixed[0:number_of // 2 * 2:2], mixed[1:number_of // 2 * 2:2]
    margin = jnp.minimum(lengths[donor] - 1, bound - lengths[receiver]) // 2
    margin = jnp.where((donor == sequence[0]) | (receiver == sequence[0]) | (lengths[receiver] == 0), 0, jnp.maximum(margin, 0))
    passed = jax.random.randint(jax.random.fold_in(own, 4), (number_of // 2,), 0, 1 << 20) % (margin + 1)
    lengths = lengths.at[donor].add(-passed).at[receiver].add(passed)
    members = jnp.searchsorted(jnp.cumsum(lengths), jnp.arange(rows * top), side="right").astype(jnp.int32)
    table = members.reshape(top, rows).T
    table = table[jax.random.permutation(jax.random.fold_in(own, 1), rows)]
    rotation = jax.random.randint(jax.random.fold_in(own, 2), (rows, 1), 0, top)
    return jnp.take_along_axis(table, (jnp.arange(top)[None, :] + rotation) % top, axis=1)


def shares(number_of, total, bound, lean, full):
    portions = [(1 << 20) // math.isqrt(grade ** lean) + 1 for grade in range(1, number_of + 1)]
    largest = bound if full else min(bound, max(-(-total // number_of), total * portions[0] // sum(portions)))
    least = 1 if total - largest >= number_of - 1 else 0
    counts, spare = [largest] + [least] * (number_of - 1), total - largest - least * (number_of - 1)
    while spare > 0:
        free = [i for i in range(1, number_of) if counts[i] < largest] or [i for i in range(1, number_of) if counts[i] < bound]
        whole, left = sum([portions[i] for i in free]), spare
        for i in free:
            more = min(bound - counts[i], max(1, left * portions[i] // whole), spare)
            counts[i] = counts[i] + more
            spare = spare - more
    return np.array(counts)


def centred(stream_key, dims, deviation, bound, cuts=(), kind=jnp.bfloat16):
    values = deviation * jax.random.normal(stream_key, dims, jnp.float32)
    if cuts:
        values = values * steps_of(stream_key, dims, cuts, -0.22, 0.18)
    return jnp.clip(values, -bound, bound).astype(kind)


def setup_inputs(seed: int = 0) -> dict:
    splits = jax.random.split(jax.random.key(seed), 6)
    grad_out = centred(splits[0], (TOKENS, D), 1.0, 6.0, ((0, 32),))
    expert_ids_keys = jax.random.split(jax.random.fold_in(splits[1], 1), TOKENS // TOK_DEV)
    expert_ids_turns = jax.random.permutation(jax.random.fold_in(splits[1], 3), TOKENS // TOK_DEV)
    expert_ids = jax.vmap(lambda own, number: shared_out(jax.random.fold_in(splits[1], 2), own, number, TOK_DEV, EXPERTS, 1, MOST, 1))(expert_ids_keys, expert_ids_turns).reshape((TOKENS, 1))
    gate_weights = jnp.clip(0.099609375 + 0.9003906 * jax.random.uniform(splits[2], (TOKENS,), jnp.float32) ** steps_of(splits[2], (TOKENS,), ((0, 32),), -0.2, 0.2), 0.099609375, 1.0).astype(jnp.bfloat16)
    saved_hidden = centred(splits[3], (EXPERTS, SLOTS, FF), 0.011, 0.06591797, ((0, 8), (2, 4)))
    down_weight = centred(splits[4], (EXPERTS, FF, D), FF ** -0.5, 0.0625, ((0, 8), (1, 4)))
    return {"grad_out": grad_out, "expert_ids": expert_ids, "gate_weights": gate_weights, "saved_hidden": saved_hidden, "down_weight": down_weight}


def reference(grad_out, expert_ids, gate_weights, saved_hidden, down_weight):
    blocks = TOKENS // TOK_DEV
    chosen = expert_ids[:, 0].astype(jnp.int32)
    grouped = chosen.reshape(blocks, TOK_DEV)
    onehot = (grouped[:, :, None] == jnp.arange(EXPERTS, dtype=jnp.int32)[None, None, :]).astype(jnp.int32)
    earlier = jnp.cumsum(onehot, axis=1) - onehot
    slot = jnp.sum(earlier * onehot, axis=2)
    position = (jnp.arange(blocks, dtype=jnp.int32)[:, None] * MOST + slot).reshape(-1).astype(jnp.int32)
    rows = jnp.zeros((EXPERTS, SLOTS, D), jnp.bfloat16).at[chosen, position].set(grad_out)
    gates = jnp.zeros((EXPERTS, SLOTS), jnp.bfloat16).at[chosen, position].set(gate_weights)

    def per_expert(items):
        expert_rows, weight, expert_gates, hidden = items
        back = jnp.dot(expert_rows, weight.T, preferred_element_type=jnp.float32)
        grad_hidden = (expert_gates.astype(jnp.float32)[:, None] * back).astype(jnp.bfloat16)
        slot_gate = jnp.sum(hidden.astype(jnp.float32) * back, axis=1)
        return grad_hidden, slot_gate

    grad_hidden, slot_gate = lax.map(per_expert, (rows, down_weight, gates, saved_hidden))
    grad_gate = slot_gate[chosen, position]
    return grad_hidden, grad_gate
```

```python
import functools
import math

import jax
import jax.numpy as jnp
from jax import lax
from jax.experimental import pallas as pl
from jax.experimental.pallas import tpu as pltpu
from jax.sharding import PartitionSpec as P

MESH = pl.DeviceIdType.MESH
F32 = jnp.float32
BF16 = jnp.bfloat16
LANES = 128
NT = (((1,), (1,)), ((), ()))


def flip(index, mask):
    out, bit = index, 1
    while bit <= mask:
        if mask & bit:
            out = out + bit * (1 - 2 * ((index // bit) % 2))
        bit *= 2
    return out


def kernel(
    dps, exps, most, parts,
    grad_hbm, ids_ref, gate_ref, hid_hbm, w_hbm,
    out_hbm, gg_ref,
    tokens, w, hid, ostage, send, raw, gsend, gts, x, gacc, psend_buf, precv_buf, total, ret,
    load_sem, out_sem, zs, zr, gzs, gzr, ps, pr, gps, gpr, rs, rr, ts, tr,
):
    d = lax.axis_index("dp")
    e = lax.axis_index("expert")
    toks = grad_hbm.shape[0]
    width = grad_hbm.shape[1]
    cols = width // parts
    block = parts * most
    rows = exps * most
    units = w.shape[0]

    loads = [
        pltpu.make_async_copy(
            grad_hbm.at[:, pl.ds(q * cols, cols)],
            tokens.at[pl.ds(q * toks, toks), :],
            load_sem.at[q],
        )
        for q in range(parts)
    ]
    loads.append(pltpu.make_async_copy(w_hbm, w, load_sem.at[parts]))
    loads.append(pltpu.make_async_copy(hid_hbm, hid, load_sem.at[parts + 1]))
    for copy in loads:
        copy.start()

    barrier = pltpu.get_barrier_semaphore()
    for k in range(1, exps):
        pl.semaphore_signal(barrier, inc=1, device_id=(d, flip(e, k)), device_id_type=MESH)
    for k in range(1, dps):
        pl.semaphore_signal(barrier, inc=1, device_id=(flip(d, k), e), device_id_type=MESH)

    ids = ids_ref[...]
    onehot = (lax.broadcasted_iota(jnp.int32, (exps, toks), 0) == ids).astype(F32)
    before = (
        lax.broadcasted_iota(jnp.int32, (toks, toks), 0)
        < lax.broadcasted_iota(jnp.int32, (toks, toks), 1)
    )
    earlier = jnp.dot(
        onehot.astype(BF16), before.astype(F32).astype(BF16), preferred_element_type=F32
    )
    slot = jnp.sum(earlier * onehot, axis=0, keepdims=True).astype(jnp.int32)
    target = ids * most + slot

    r4 = lax.broadcasted_iota(jnp.int32, (block, parts * toks), 0)
    c4 = lax.broadcasted_iota(jnp.int32, (block, parts * toks), 1)
    same_part = (r4 // most) == (c4 // toks)
    r_slot = r4 % most
    target4 = jnp.concatenate([target] * parts, axis=1)
    lane_slot = lax.broadcasted_iota(jnp.int32, (LANES, toks), 0)
    gate_rows = jnp.broadcast_to(gate_ref[...].astype(F32), (16, toks)).astype(BF16)

    def block_for(dest):
        place = jnp.where(same_part & (r_slot + dest * most == target4), 1.0, 0.0).astype(BF16)
        return jnp.dot(place, tokens[...], preferred_element_type=F32).astype(BF16)

    def gates_for(dest):
        hit = (lane_slot < most) & (lane_slot + dest * most == target)
        place = jnp.where(hit, 1.0, 0.0).astype(BF16)
        return lax.dot_general(gate_rows, place, NT, preferred_element_type=F32).astype(BF16)

    def z_copy(k):
        dest = flip(e, k)
        return pltpu.make_async_remote_copy(
            src_ref=send.at[k], dst_ref=raw.at[d, e], send_sem=zs.at[k], recv_sem=zr.at[e],
            device_id=(d, dest), device_id_type=MESH,
        )

    def z_gate(k):
        dest = flip(e, k)
        return pltpu.make_async_remote_copy(
            src_ref=gsend.at[k], dst_ref=gts.at[d, e], send_sem=gzs.at[k], recv_sem=gzr.at[e],
            device_id=(d, dest), device_id_type=MESH,
        )

    def plane_copy(of, via, k, j):
        s = flip(e, k)
        src = flip(d, of)
        return pltpu.make_async_remote_copy(
            src_ref=raw.at[src, s], dst_ref=raw.at[src, s], send_sem=ps.at[j, k],
            recv_sem=pr.at[src, s], device_id=(flip(d, via), e), device_id_type=MESH,
        )

    def z_wait(k):
        s = flip(e, k)
        pltpu.make_async_remote_copy(
            src_ref=send.at[k], dst_ref=raw.at[d, s], send_sem=zs.at[k], recv_sem=zr.at[s],
            device_id=(d, s), device_id_type=MESH,
        ).wait_recv()

    def gate_wait(k):
        s = flip(e, k)
        pltpu.make_async_remote_copy(
            src_ref=gsend.at[k], dst_ref=gts.at[d, s], send_sem=gzs.at[k], recv_sem=gzr.at[s],
            device_id=(d, s), device_id_type=MESH,
        ).wait_recv()

    def plane_gate(k):
        return pltpu.make_async_remote_copy(
            src_ref=gts.at[d], dst_ref=gts.at[d], send_sem=gps.at[k], recv_sem=gpr.at[d],
            device_id=(flip(d, k), e), device_id_type=MESH,
        )

    def plane_gate_wait(k):
        src = flip(d, k)
        pltpu.make_async_remote_copy(
            src_ref=gts.at[d], dst_ref=gts.at[src], send_sem=gps.at[k], recv_sem=gpr.at[src],
            device_id=(src, e), device_id_type=MESH,
        ).wait_recv()

    def sum_copy(k):
        return pltpu.make_async_remote_copy(
            src_ref=psend_buf.at[k], dst_ref=precv_buf.at[k], send_sem=rs.at[k],
            recv_sem=rr.at[k], device_id=(flip(d, k), e), device_id_type=MESH,
        )

    def back_copy(k):
        return pltpu.make_async_remote_copy(
            src_ref=total, dst_ref=ret.at[k], send_sem=ts.at[k], recv_sem=tr.at[k],
            device_id=(d, flip(e, k)), device_id_type=MESH,
        )

    for copy in loads[:parts]:
        copy.wait()
    pl.semaphore_wait(barrier, exps - 1 + dps - 1)

    forwards = dps == 4
    started = []

    def start(copy):
        copy.start()
        started.append(copy)

    def plane_start(k):
        for j in ([1, 2] if forwards else range(1, dps)):
            start(plane_copy(0, j, k, j))

    waited = set()

    def plane_wait(of, k):
        if (of, k) not in waited:
            waited.add((of, k))
            plane_copy(of, of, k, of).wait_recv()

    def forward(k):
        first, then = (1, 2) if k % 2 == 0 else (2, 1)
        plane_wait(first, k)
        start(plane_copy(first, then, k, 3))

    raw[d, e] = block_for(e)
    plane_start(0)
    for k in range(1, exps):
        send[k] = block_for(flip(e, k))
        start(z_copy(k))
    gts[d, e] = gates_for(e)
    for k in range(1, exps):
        gsend[k] = gates_for(flip(e, k))
        start(z_gate(k))

    lag = 2
    for k in range(1, exps):
        z_wait(k)
        plane_start(k)
        if forwards and k >= lag:
            forward(k - lag)
    for k in range(1, exps):
        gate_wait(k)
    for k in range(1, dps):
        start(plane_gate(k))
    loads[parts].wait()
    loads[parts + 1].wait()

    def unpack(at, k):
        src = flip(d, k)
        for g in range(exps // parts):
            arrived = raw[src, pl.ds(g * parts, parts)].reshape(parts * block, cols)
            rr_ = lax.broadcasted_iota(jnp.int32, (block, parts * block), 0)
            cc_ = lax.broadcasted_iota(jnp.int32, (block, parts * block), 1)
            base = (rr_ // most) * block + rr_ % most
            for q in range(parts):
                pick = jnp.where(cc_ == base + q * most, 1.0, 0.0).astype(BF16)
                x[pl.ds(at * rows + g * block, block), pl.ds(q * cols, cols)] = jnp.dot(
                    pick, arrived, preferred_element_type=F32
                ).astype(BF16)

    lane_of = lax.broadcasted_iota(jnp.int32, (rows, LANES), 1)
    row_of = lax.broadcasted_iota(jnp.int32, (rows, LANES), 0)
    own_lane = lane_of == row_of % most

    def gate_column(k):
        src = flip(d, k)
        pick = jnp.where(
            lax.broadcasted_iota(jnp.int32, (rows, exps * 16), 1)
            == (lax.broadcasted_iota(jnp.int32, (rows, exps * 16), 0) // most) * 16,
            1.0, 0.0,
        ).astype(BF16)
        spread = jnp.dot(pick, gts[src].reshape(exps * 16, LANES), preferred_element_type=F32)
        return jnp.sum(jnp.where(own_lane, spread, 0.0), axis=1, keepdims=True)

    tile = min(256, units)
    outs = []

    def compute(ks):
        m = len(ks) * rows
        gates = [gate_column(k) for k in ks]
        starts = [pl.multiple_of(flip(d, k) * rows, 16) for k in ks]
        gacc[pl.ds(0, m), :] = jnp.zeros((m, LANES), F32)

        def body(n, carry):
            at = pl.multiple_of(n * tile, tile)
            back = lax.dot_general(
                x[pl.ds(0, m), :], w[pl.ds(at, tile), :], NT, preferred_element_type=F32
            )
            for i in range(len(ks)):
                part = back[i * rows:(i + 1) * rows]
                ostage[pl.ds(starts[i], rows), pl.ds(at, tile)] = (gates[i] * part).astype(BF16)
                prod = hid[pl.ds(starts[i], rows), pl.ds(at, tile)].astype(F32) * part
                summed = prod[:, :LANES]
                for c in range(1, tile // LANES):
                    summed = summed + prod[:, c * LANES:(c + 1) * LANES]
                gacc[pl.ds(i * rows, rows), :] += summed
            return carry

        lax.fori_loop(0, units // tile, body, 0)
        for i, k in enumerate(ks):
            copy = pltpu.make_async_copy(
                ostage.at[pl.ds(starts[i], rows), :], out_hbm.at[pl.ds(starts[i], rows), :],
                out_sem.at[k],
            )
            copy.start()
            outs.append(copy)
            value = jnp.sum(gacc[pl.ds(i * rows, rows), :], axis=1, keepdims=True)
            spread = jnp.where(own_lane, value, 0.0)
            pick = jnp.where(
                lax.broadcasted_iota(jnp.int32, (exps, rows), 0)
                == lax.broadcasted_iota(jnp.int32, (exps, rows), 1) // most,
                1.0, 0.0,
            )
            psend_buf[k] = jnp.dot(
                pick, spread, preferred_element_type=F32, precision=lax.Precision.HIGHEST
            )
            if k:
                start(sum_copy(k))

    unpack(0, 0)
    if forwards:
        for k in range(exps - lag, exps - 1):
            forward(k)
    compute([0])
    if forwards:
        forward(exps - 1)
    order = list(range(1, dps))
    groups = [order[i:i + 2] for i in range(0, len(order), 2)]
    for group in groups:
        for i, k in enumerate(group):
            plane_gate_wait(k)
            for j in range(exps):
                plane_wait(k, j)
            unpack(i, k)
        compute(group)

    summed = psend_buf[0]
    for k in range(1, dps):
        sum_copy(k).wait_recv()
        summed = summed + precv_buf[k]
    total[...] = summed
    for k in range(1, exps):
        start(back_copy(k))
    erow = lax.broadcasted_iota(jnp.int32, (exps, LANES), 0)
    returned = jnp.zeros((exps, LANES), F32)
    for k in range(exps):
        if k:
            back_copy(k).wait_recv()
            piece = ret[k]
        else:
            piece = summed
        mine = jnp.sum(jnp.where(erow == e, piece, 0.0), axis=0, keepdims=True)
        returned = jnp.where(erow == flip(e, k), mine, returned)
    pick = jnp.where(lax.broadcasted_iota(jnp.int32, (LANES, toks), 0) == slot, 1.0, 0.0)
    spread = jnp.dot(
        returned, pick, preferred_element_type=F32, precision=lax.Precision.HIGHEST
    )
    gg_ref[...] = jnp.sum(spread * onehot, axis=0, keepdims=True)
    for copy in outs:
        copy.wait()
    for copy in started:
        copy.wait_send()


def shards(dps, exps, grad_out, expert_ids, gate_weights, saved_hidden, down_weight):
    toks, width = grad_out.shape
    units = down_weight.shape[1]
    slots = saved_hidden.shape[1]
    most = slots // (dps * exps)
    parts = 16 // math.gcd(most, 16)
    block, cols, rows = parts * most, width // parts, exps * most
    vmem, dma = pltpu.VMEM, pltpu.SemaphoreType.DMA
    any_spec = pl.BlockSpec(memory_space=pl.ANY)
    vm_spec = pl.BlockSpec(memory_space=pltpu.VMEM)
    hidden, gate = pl.pallas_call(
        functools.partial(kernel, dps, exps, most, parts),
        out_shape=(
            jax.ShapeDtypeStruct((slots, units), BF16),
            jax.ShapeDtypeStruct((1, toks), F32),
        ),
        in_specs=[any_spec, vm_spec, vm_spec, any_spec, any_spec],
        out_specs=(any_spec, vm_spec),
        scratch_shapes=[
            vmem((parts * toks, cols), BF16),
            vmem((units, width), BF16),
            vmem((slots, units), BF16),
            vmem((slots, units), BF16),
            vmem((exps, block, cols), BF16),
            vmem((dps, exps, block, cols), BF16),
            vmem((exps, 16, LANES), BF16),
            vmem((dps, exps, 16, LANES), BF16),
            vmem((2 * rows, width), BF16),
            vmem((2 * rows, LANES), F32),
            vmem((dps, exps, LANES), F32),
            vmem((dps, exps, LANES), F32),
            vmem((exps, LANES), F32),
            vmem((exps, exps, LANES), F32),
            dma((parts + 2,)),
            dma((dps,)),
            dma((exps,)), dma((exps,)),
            dma((exps,)), dma((exps,)),
            dma((dps, exps)), dma((dps, exps)),
            dma((dps,)), dma((dps,)),
            dma((dps,)), dma((dps,)),
            dma((exps,)), dma((exps,)),
        ],
        compiler_params=pltpu.CompilerParams(
            collective_id=0, has_side_effects=True, vmem_limit_bytes=58 * 1024 * 1024
        ),
    )(
        grad_out,
        expert_ids.reshape(1, toks),
        gate_weights.reshape(1, toks),
        saved_hidden[0],
        down_weight[0],
    )
    return hidden[None], gate.reshape(toks)


def solution(mesh):
    in_specs = (
        P(("dp", "expert"), None),
        P(("dp", "expert"), None),
        P(("dp", "expert")),
        P("expert", None, "dp"),
        P("expert", "dp", None),
    )
    out_specs = (P("expert", None, "dp"), P(("dp", "expert")))
    body = functools.partial(shards, mesh.shape["dp"], mesh.shape["expert"])
    return jax.shard_map(body, mesh=mesh, in_specs=in_specs, out_specs=out_specs, check_vma=False)
```

```python
import functools
import math

import jax
import jax.numpy as jnp
from jax import lax
from jax.experimental import pallas as pl
from jax.experimental.pallas import tpu as pltpu
from jax.sharding import PartitionSpec as P

MESH = pl.DeviceIdType.MESH
F32 = jnp.float32
BF16 = jnp.bfloat16
LANES = 128
CHUNKS = (768, 512)
NT = (((1,), (1,)), ((), ()))


def flip(index, mask):
    out, bit = index, 1
    while bit <= mask:
        if mask & bit:
            out = out + bit * (1 - 2 * ((index // bit) % 2))
        bit *= 2
    return out


def kernel(
    dps, exps, most, parts, chunks,
    grad_hbm, ids_ref, gate_ref, hid_hbm, w_hbm,
    out_hbm, gg_ref,
    tokens, w, hid, ostage, *rest,
):
    n = len(chunks)
    send, raw = rest[:n], rest[n:2 * n]
    (
        acc, gsend, gts, x, gacc, psend_buf, precv_buf, total, ret,
        load_sem, out_sem, zs, zr, gzs, gzr, ps, pr, gps, gpr, rs, rr, ts, tr,
    ) = rest[2 * n:]
    offsets = [sum(chunks[:c]) for c in range(n)]
    d = lax.axis_index("dp")
    e = lax.axis_index("expert")
    toks = grad_hbm.shape[0]
    width = grad_hbm.shape[1]
    cols = width // parts
    block = parts * most
    rows = exps * most
    units = w.shape[0]

    loads = [
        pltpu.make_async_copy(
            grad_hbm.at[:, pl.ds(q * cols, cols)],
            tokens.at[pl.ds(q * toks, toks), :],
            load_sem.at[q],
        )
        for q in range(parts)
    ]
    loads.append(pltpu.make_async_copy(w_hbm, w, load_sem.at[parts]))
    loads.append(pltpu.make_async_copy(hid_hbm, hid, load_sem.at[parts + 1]))
    for copy in loads[:parts]:
        copy.start()

    barrier = pltpu.get_barrier_semaphore()
    for k in range(1, exps):
        pl.semaphore_signal(barrier, inc=1, device_id=(d, flip(e, k)), device_id_type=MESH)
    for k in range(1, dps):
        pl.semaphore_signal(barrier, inc=1, device_id=(flip(d, k), e), device_id_type=MESH)

    ids = ids_ref[...]
    onehot = (lax.broadcasted_iota(jnp.int32, (exps, toks), 0) == ids).astype(F32)
    before = (
        lax.broadcasted_iota(jnp.int32, (toks, toks), 0)
        < lax.broadcasted_iota(jnp.int32, (toks, toks), 1)
    )
    earlier = jnp.dot(
        onehot.astype(BF16), before.astype(F32).astype(BF16), preferred_element_type=F32
    )
    slot = jnp.sum(earlier * onehot, axis=0, keepdims=True).astype(jnp.int32)
    target = ids * most + slot

    r4 = lax.broadcasted_iota(jnp.int32, (block, parts * toks), 0)
    c4 = lax.broadcasted_iota(jnp.int32, (block, parts * toks), 1)
    same_part = (r4 // most) == (c4 // toks)
    r_slot = r4 % most
    target4 = jnp.concatenate([target] * parts, axis=1)
    lane_slot = lax.broadcasted_iota(jnp.int32, (LANES, toks), 0)
    gate_rows = jnp.broadcast_to(gate_ref[...].astype(F32), (16, toks)).astype(BF16)

    def block_for(dest, c):
        place = jnp.where(same_part & (r_slot + dest * most == target4), 1.0, 0.0).astype(BF16)
        return jnp.dot(
            place, tokens[:, offsets[c]:offsets[c] + chunks[c]], preferred_element_type=F32
        ).astype(BF16)

    def gates_for(dest):
        hit = (lane_slot < most) & (lane_slot + dest * most == target)
        place = jnp.where(hit, 1.0, 0.0).astype(BF16)
        return lax.dot_general(gate_rows, place, NT, preferred_element_type=F32).astype(BF16)

    def z_copy(c, k):
        dest = flip(e, k)
        return pltpu.make_async_remote_copy(
            src_ref=send[c].at[k], dst_ref=raw[c].at[d, e], send_sem=zs.at[c, k],
            recv_sem=zr.at[c, e],
            device_id=(d, dest), device_id_type=MESH,
        )

    def z_gate(k):
        dest = flip(e, k)
        return pltpu.make_async_remote_copy(
            src_ref=gsend.at[k], dst_ref=gts.at[d, e], send_sem=gzs.at[k], recv_sem=gzr.at[e],
            device_id=(d, dest), device_id_type=MESH,
        )

    def plane_copy(of, via, c, k, j):
        s = flip(e, k)
        src = flip(d, of)
        return pltpu.make_async_remote_copy(
            src_ref=raw[c].at[src, s], dst_ref=raw[c].at[src, s], send_sem=ps.at[c, j, k],
            recv_sem=pr.at[c, src, s], device_id=(flip(d, via), e), device_id_type=MESH,
        )

    def z_wait(c, k):
        s = flip(e, k)
        pltpu.make_async_remote_copy(
            src_ref=send[c].at[k], dst_ref=raw[c].at[d, s], send_sem=zs.at[c, k],
            recv_sem=zr.at[c, s],
            device_id=(d, s), device_id_type=MESH,
        ).wait_recv()

    def gate_wait(k):
        s = flip(e, k)
        pltpu.make_async_remote_copy(
            src_ref=gsend.at[k], dst_ref=gts.at[d, s], send_sem=gzs.at[k], recv_sem=gzr.at[s],
            device_id=(d, s), device_id_type=MESH,
        ).wait_recv()

    def plane_gate(k):
        return pltpu.make_async_remote_copy(
            src_ref=gts.at[d], dst_ref=gts.at[d], send_sem=gps.at[k], recv_sem=gpr.at[d],
            device_id=(flip(d, k), e), device_id_type=MESH,
        )

    def plane_gate_wait(k):
        src = flip(d, k)
        pltpu.make_async_remote_copy(
            src_ref=gts.at[d], dst_ref=gts.at[src], send_sem=gps.at[k], recv_sem=gpr.at[src],
            device_id=(src, e), device_id_type=MESH,
        ).wait_recv()

    def sum_copy(k):
        return pltpu.make_async_remote_copy(
            src_ref=psend_buf.at[k], dst_ref=precv_buf.at[k], send_sem=rs.at[k],
            recv_sem=rr.at[k], device_id=(flip(d, k), e), device_id_type=MESH,
        )

    def back_copy(k):
        return pltpu.make_async_remote_copy(
            src_ref=total, dst_ref=ret.at[k], send_sem=ts.at[k], recv_sem=tr.at[k],
            device_id=(d, flip(e, k)), device_id_type=MESH,
        )

    for copy in loads[:parts]:
        copy.wait()
    for copy in loads[parts:]:
        copy.start()
    raw[0][d, e] = block_for(e, 0)
    pl.semaphore_wait(barrier, exps - 1 + dps - 1)

    forwards = dps == 4
    started = []

    def start(copy):
        copy.start()
        started.append(copy)

    def plane_start(c, k):
        for j in ([1, 2] if forwards else range(1, dps)):
            start(plane_copy(0, j, c, k, j))

    waited = set()

    def plane_wait(of, c, k):
        if (of, c, k) not in waited:
            waited.add((of, c, k))
            plane_copy(of, of, c, k, of).wait_recv()

    def forward(c, k):
        first, then = (1, 2) if k % 2 == 0 else (2, 1)
        plane_wait(first, c, k)
        start(plane_copy(first, then, c, k, 3))

    lane_of = lax.broadcasted_iota(jnp.int32, (block, LANES), 1)
    row_of = lax.broadcasted_iota(jnp.int32, (block, LANES), 0)
    own_lane = lane_of == row_of % most
    tile = min(512 if dps <= 4 else 256, units)
    half = dps * block
    outs = []

    def group(h):
        return flip(e // parts, h)

    def unpack(c, h):
        for k in range(dps):
            for j in range(parts):
                if k:
                    plane_wait(k, c, h * parts + j)
        wide = chunks[c]
        for k in range(dps):
            arrived = raw[c][flip(d, k), pl.ds(group(h) * parts, parts)]
            arrived = arrived.reshape(parts * block, wide)
            rows_ = lax.broadcasted_iota(jnp.int32, (block, parts * block), 0)
            cols_ = lax.broadcasted_iota(jnp.int32, (block, parts * block), 1)
            base = (rows_ // most) * block + rows_ % most
            for q in range(parts):
                pick = jnp.where(cols_ == base + q * most, 1.0, 0.0).astype(BF16)
                x[pl.ds(k * block, block), pl.ds(q * wide, wide)] = jnp.dot(
                    pick, arrived, preferred_element_type=F32
                ).astype(BF16)

    def row_start(h, k):
        return pl.multiple_of(flip(d, k) * rows + group(h) * block, 16)

    def gate_column(h, k):
        pick = jnp.where(
            lax.broadcasted_iota(jnp.int32, (block, parts * 16), 1)
            == (lax.broadcasted_iota(jnp.int32, (block, parts * 16), 0) // most) * 16,
            1.0, 0.0,
        ).astype(BF16)
        tiles = gts[flip(d, k), pl.ds(group(h) * parts, parts)].reshape(parts * 16, LANES)
        spread = jnp.dot(pick, tiles, preferred_element_type=F32)
        return jnp.sum(jnp.where(own_lane, spread, 0.0), axis=1, keepdims=True)

    def compute(c, h, step, gates):
        cols_at = pl.ds(step * tile, tile)
        wide = chunks[c]
        pieces = [w[cols_at, pl.ds(q * cols + offsets[c], wide)] for q in range(parts)]
        weight = jnp.concatenate(pieces, axis=1) if n > 1 else w[cols_at, :]
        back = lax.dot_general(
            x[:, pl.ds(0, parts * wide)], weight, NT, preferred_element_type=F32
        )
        if c:
            back = back + acc[h, :, cols_at]
        if c < n - 1:
            acc[h, :, cols_at] = back
            return
        for k in range(dps):
            part = back[k * block:(k + 1) * block]
            at = pl.ds(row_start(h, k), block)
            ostage[at, cols_at] = (gates[k] * part).astype(BF16)
            prod = hid[at, cols_at].astype(F32) * part
            summed = prod[:, :LANES]
            for i in range(1, tile // LANES):
                summed = summed + prod[:, i * LANES:(i + 1) * LANES]
            if step:
                summed = summed + gacc[h, pl.ds(k * block, block), :]
            gacc[h, pl.ds(k * block, block), :] = summed

    def finish(h):
        for k in range(dps):
            at = pl.ds(row_start(h, k), block)
            copy = pltpu.make_async_copy(ostage.at[at, :], out_hbm.at[at, :], out_sem.at[h, k])
            copy.start()
            outs.append(copy)
        for k in list(range(1, dps)) + [0]:
            value = jnp.sum(gacc[h, pl.ds(k * block, block), :], axis=1, keepdims=True)
            spread = jnp.where(own_lane, value, 0.0)
            pick = jnp.where(
                lax.broadcasted_iota(jnp.int32, (exps, block), 0)
                == group(h) * parts + lax.broadcasted_iota(jnp.int32, (exps, block), 1) // most,
                1.0, 0.0,
            )
            share = jnp.dot(
                pick, spread, preferred_element_type=F32, precision=lax.Precision.HIGHEST
            )
            psend_buf[k] = psend_buf[k] + share if h else share
            if h == halves - 1 and k:
                start(sum_copy(k))

    halves = exps // parts
    steps = units // tile
    work = []
    gates = {}

    def gates_ready():
        loads[parts + 1].wait()
        for k in range(1, dps):
            plane_gate_wait(k)

    def prepare(c, h):
        if c == n - 1:
            gates[h] = [gate_column(h, k) for k in range(dps)]
        unpack(c, h)

    for c in range(n):
        for h in range(halves):
            for step in range(steps):
                work.append((c, h, step))

    def do_work():
        c, h, step = work.pop(0)
        if step == 0:
            if c == 0 and h == 0:
                loads[parts].wait()
            if c == n - 1 and h == 0:
                gates_ready()
            prepare(c, h)
        compute(c, h, step, gates.get(h))
        if c == n - 1 and step == steps - 1:
            finish(h)

    plane_start(0, 0)
    for c in range(n):
        for k in range(exps):
            if k:
                send[c][k] = block_for(flip(e, k), c)
                start(z_copy(c, k))
            elif c:
                raw[c][d, e] = block_for(e, c)
        if c == 0:
            gts[d, e] = gates_for(e)
            for k in range(1, exps):
                gsend[k] = gates_for(flip(e, k))
                start(z_gate(k))

    lag = 2
    order = [(c, k) for c in range(n) for k in range(exps)]
    for i, (c, k) in enumerate(order):
        if i:
            if k:
                z_wait(c, k)
            plane_start(c, k)
        if i == exps - 1:
            for k_ in range(1, exps):
                gate_wait(k_)
            for k_ in range(1, dps):
                start(plane_gate(k_))
        if forwards:
            if i >= lag:
                forward(*order[i - lag])
            if i >= exps and n > 1:
                do_work()
    if forwards:
        for i in range(lag, 0, -1):
            forward(*order[-i])
            if n > 1:
                do_work()
    while work:
        do_work()

    summed = psend_buf[0]
    for k in range(1, dps):
        sum_copy(k).wait_recv()
        summed = summed + precv_buf[k]
    total[...] = summed
    for k in range(1, exps):
        start(back_copy(k))
    erow = lax.broadcasted_iota(jnp.int32, (exps, LANES), 0)
    returned = jnp.zeros((exps, LANES), F32)
    for k in range(exps):
        if k:
            back_copy(k).wait_recv()
            piece = ret[k]
        else:
            piece = summed
        mine = jnp.sum(jnp.where(erow == e, piece, 0.0), axis=0, keepdims=True)
        returned = jnp.where(erow == flip(e, k), mine, returned)
    pick = jnp.where(lax.broadcasted_iota(jnp.int32, (LANES, toks), 0) == slot, 1.0, 0.0)
    spread = jnp.dot(
        returned, pick, preferred_element_type=F32, precision=lax.Precision.HIGHEST
    )
    gg_ref[...] = jnp.sum(spread * onehot, axis=0, keepdims=True)
    for copy in outs:
        copy.wait()
    for copy in started:
        copy.wait_send()


def shards(dps, exps, grad_out, expert_ids, gate_weights, saved_hidden, down_weight):
    toks, width = grad_out.shape
    units = down_weight.shape[1]
    slots = saved_hidden.shape[1]
    most = slots // (dps * exps)
    parts = 16 // math.gcd(most, 16)
    block, cols = parts * most, width // parts
    chunks = CHUNKS if sum(CHUNKS) == cols else (cols,)
    n = len(chunks)
    vmem, dma = pltpu.VMEM, pltpu.SemaphoreType.DMA
    any_spec = pl.BlockSpec(memory_space=pl.ANY)
    vm_spec = pl.BlockSpec(memory_space=pltpu.VMEM)
    hidden, gate = pl.pallas_call(
        functools.partial(kernel, dps, exps, most, parts, chunks),
        out_shape=(
            jax.ShapeDtypeStruct((slots, units), BF16),
            jax.ShapeDtypeStruct((1, toks), F32),
        ),
        in_specs=[any_spec, vm_spec, vm_spec, any_spec, any_spec],
        out_specs=(any_spec, vm_spec),
        scratch_shapes=[
            vmem((parts * toks, cols), BF16),
            vmem((units, width), BF16),
            vmem((slots, units), BF16),
            vmem((slots, units), BF16),
            *[vmem((exps, block, wide), BF16) for wide in chunks],
            *[vmem((dps, exps, block, wide), BF16) for wide in chunks],
            vmem((exps // parts, dps * block, units) if n > 1 else (1, 8, LANES), F32),
            vmem((exps, 16, LANES), BF16),
            vmem((dps, exps, 16, LANES), BF16),
            vmem((dps * block, parts * max(chunks)), BF16),
            vmem((exps // parts, dps * block, LANES), F32),
            vmem((dps, exps, LANES), F32),
            vmem((dps, exps, LANES), F32),
            vmem((exps, LANES), F32),
            vmem((exps, exps, LANES), F32),
            dma((parts + 2,)),
            dma((exps // parts, dps)),
            dma((n, exps)), dma((n, exps)),
            dma((exps,)), dma((exps,)),
            dma((n, dps, exps)), dma((n, dps, exps)),
            dma((dps,)), dma((dps,)),
            dma((dps,)), dma((dps,)),
            dma((exps,)), dma((exps,)),
        ],
        compiler_params=pltpu.CompilerParams(
            collective_id=0, has_side_effects=True, vmem_limit_bytes=58 * 1024 * 1024
        ),
    )(
        grad_out,
        expert_ids.reshape(1, toks),
        gate_weights.reshape(1, toks),
        saved_hidden[0],
        down_weight[0],
    )
    return hidden[None], gate.reshape(toks)


def solution(mesh):
    in_specs = (
        P(("dp", "expert"), None),
        P(("dp", "expert"), None),
        P(("dp", "expert")),
        P("expert", None, "dp"),
        P("expert", "dp", None),
    )
    out_specs = (P("expert", None, "dp"), P(("dp", "expert")))
    body = functools.partial(shards, mesh.shape["dp"], mesh.shape["expert"])
    return jax.shard_map(body, mesh=mesh, in_specs=in_specs, out_specs=out_specs, check_vma=False)
```
